32 devices in a mesh: grp: 2 (over y), node: 4 (over x, core), chip: 4 (over z).
Axes of the slice: x: 2, y: 2, z: 4, core: 2. Of those that a mesh axis runs over, the one named last changes fastest.
Arguments:
- tokens: bfloat16 [4096, 7168], P(('grp', 'node', 'chip')), parts along dimension 0, may hold values from -31 to 31
- norm_gain: float32 [7168], replicated, may hold values from 0.1 to 1.9
- expert_ids: int32 [4096, 8], P(('grp', 'node', 'chip')), parts along dimension 0, may hold values from 0 to 383, as said below
- gate_num: int32 [4096, 8], P(('grp', 'node', 'chip')), parts along dimension 0, may hold values from 1 to 4096
- node_mask: int32 [4096, 4], P(('grp', 'node', 'chip')), parts along dimension 0, may hold values from 0 to 1, as said below
- w_gate: bfloat16 [4, 7168, 1024], P('node', 'chip'), may hold values from -0.0625 to 0.0625
- w_up: bfloat16 [4, 7168, 1024], P('node', 'chip'), may hold values from -0.0625 to 0.0625
- w_down: bfloat16 [4, 1024, 7168], P('node', None, 'chip'), may hold values from -0.1875 to 0.1875
Outputs:
- mixed: bfloat16 [4096, 7168], P(('grp', 'node', 'chip')), parts along dimension 0
The draws below stay inside these ranges and needn't reach their ends.
There are 2 independent parts, one for each index of `grp`. The reference program is written for one: setup_inputs(seed, part) draws one part's arguments, and reference() takes and returns one part's arrays. A program takes and returns all parts, laid end to end along the dimension named above; an argument that names none is the same for every part. Nothing has to cross between parts.
Inputs may be any that keep to these rules, and one draw needn't show every extreme that they name: `expert_ids`: each row names 8 different experts; expert e lives on node e // 96, and a row's experts lie on at most 4 nodes. Exactly one id of each row is a multiple of 96. Among the 128 rows of one device no such id is named more than 64 times. `node_mask`: each row has at most 4 ones, all at nodes of the row's experts.
All inputs are finite; a program needn't handle non-finite values.
Results may differ from the reference program's by a relative error of at most 0.0038.
Values may be sent and summed in bfloat16 or wider, within the bound.
A program may use at most 128 MiB of HBM per device.

```python
import math
import jax
import jax.numpy as jnp
from jax import lax

D = 7168
FF = 1024
TOPK = 8
DEN = 4096
TOK_DEV = 128
TOKENS = 2048
EXP_NODE = 96
NODE_TOP = 4
CAP = 64
N_NODE = 4


def routing_table(key):
    blocks = TOKENS // TOK_DEV
    subkeys = jax.random.split(key, 8)
    busiest = jax.random.randint(subkeys[0], (), 0, N_NODE)
    second = jax.random.randint(subkeys[1], (blocks, 1), CAP // 2, CAP + 1)
    places = jax.vmap(lambda item: jax.random.permutation(item, TOK_DEV))(jax.random.split(subkeys[2], blocks))
    spread = jnp.maximum(places - CAP - second, 0) % (N_NODE - 2)
    load_rank = jnp.where(places < CAP, 0, jnp.where(places < CAP + second, 1, 2 + spread))
    shuffle = jax.vmap(lambda item: jax.random.permutation(item, N_NODE - 1))(jax.random.split(subkeys[3], blocks))
    offset = jnp.take_along_axis(shuffle, jnp.maximum(load_rank - 1, 0), axis=1)
    target_node = jnp.where(load_rank == 0, busiest, (busiest + 1 + offset) % N_NODE).reshape(TOKENS)
    scores = jax.random.randint(subkeys[4], (TOKENS, N_NODE - 1), 0, 1 << 20) * (N_NODE - 1) + jnp.arange(N_NODE - 1)
    chosen = jnp.argsort(scores, axis=1)[:, :NODE_TOP - 1]
    node_set = jnp.concatenate([target_node[:, None], (target_node[:, None] + 1 + chosen) % N_NODE], axis=1)
    local_base = jax.random.randint(subkeys[5], (TOKENS, NODE_TOP), 0, EXP_NODE - 1)
    columns = [target_node * EXP_NODE]
    for column in range(1, TOPK):
        member_idx = column % NODE_TOP
        repeat = column // NODE_TOP
        local_idx = 1 + (local_base[:, member_idx] + repeat) % (EXP_NODE - 1)
        columns.append(node_set[:, member_idx] * EXP_NODE + local_idx)
    experts = jnp.stack(columns, axis=1)
    shuffle_cols = jax.random.randint(subkeys[6], (TOKENS, TOPK), 0, 1 << 20) * TOPK + jnp.arange(TOPK)
    experts = jnp.take_along_axis(experts, jnp.argsort(shuffle_cols, axis=1), axis=1)
    flat_rank = load_rank.reshape(TOKENS)
    retained = jnp.where(flat_rank == 0, 1, (jax.random.randint(subkeys[7], (TOKENS,), 0, 4) > 0).astype(jnp.int32))
    node_ids = jnp.arange(N_NODE)
    membership = jnp.sum((node_set[:, :, None] == node_ids[None, None, :]).astype(jnp.int32), axis=1)
    membership = membership * jnp.where(node_ids[None, :] == target_node[:, None], retained[:, None], 1)
    return (experts.astype(jnp.int32), membership.astype(jnp.int32))


def draw_expert_ids(key, part):
    experts, membership = routing_table(key)
    return experts


def draw_node_mask(key, part):
    experts, membership = routing_table(key)
    return membership


def draw_tokens(key, part):
    key = jax.random.fold_in(key, 11)
    first_key, second_key, third_key = jax.random.split(key, 3)
    row_scale = jnp.exp(jax.random.uniform(first_key, (TOKENS, 1), jnp.float32, 0.0, math.log(3.2)))
    col_scale = jnp.exp(jax.random.uniform(second_key, (1, D), jnp.float32, 0.0, math.log(3.2)))
    values = jax.random.truncated_normal(third_key, -3.0, 3.0, (TOKENS, D), jnp.float32)
    return (values * row_scale * col_scale).astype(jnp.bfloat16)


def place_ends(drawn, stream_key, smallest, high):
    dims = drawn.shape
    index_at = [jax.random.randint(jax.random.fold_in(stream_key, axis), (), 0, dims[axis]) for axis in range(len(dims))]
    drawn = drawn.at[tuple(index_at)].set(smallest)
    longest = dims.index(max(dims))
    index_at[longest] = (index_at[longest] + 1) % dims[longest]
    return drawn.at[tuple(index_at)].set(high)


def block_levels(key, shape, shards, low, high):
    loudness, own = 1.0, jax.random.fold_in(key, 6)
    for dim, shards_of in shards:
        steps = jnp.exp(jax.random.uniform(jax.random.fold_in(own, dim), (shards_of,), jnp.float32, low / len(shards), high / len(shards)))
        loudness = loudness * jnp.repeat(steps, shape[dim] // shards_of).reshape([-1 if axis == dim else 1 for axis in range(len(shape))])
    return loudness


def normal_values(own_key, dims, scale, bound, cuts=(), held_as=jnp.bfloat16):
    array = jax.random.normal(own_key, dims, jnp.float32) * scale
    if len(cuts) > 0:
        array = block_levels(own_key, dims, cuts, -0.22, 0.18) * array
    return jnp.clip(array, min=-bound, max=bound).astype(held_as)


def setup_inputs(seed: int = 0, part: int = 0) -> dict:
    splits = jax.random.split(jax.random.key(seed), 9)
    own_keys = jax.random.split(jax.random.fold_in(splits[8], part), 9)
    return {
        "tokens": draw_tokens(jax.random.fold_in(jax.random.fold_in(splits[8], part), 71), part),
        "norm_gain": jnp.clip(1.0 + 0.18 * jax.random.normal(splits[1], (D,), jnp.float32), 0.1, 1.9),
        "expert_ids": draw_expert_ids(jax.random.fold_in(jax.random.fold_in(splits[8], part), 71), part),
        "gate_num": place_ends(jax.random.randint(own_keys[3], (TOKENS, TOPK), 1, DEN + 1), jax.random.fold_in(own_keys[3], 1), 1, DEN).astype(jnp.int32),
        "node_mask": draw_node_mask(jax.random.fold_in(jax.random.fold_in(splits[8], part), 71), part),
        "w_gate": normal_values(splits[5], (N_NODE, D, FF), D ** -0.5, 0.0625, ((0, 4), (1, 4))),
        "w_up": normal_values(splits[6], (N_NODE, D, FF), D ** -0.5, 0.0625, ((0, 4), (1, 4))),
        "w_down": normal_values(splits[7], (N_NODE, FF, D), FF ** -0.5, 0.1875, ((0, 4), (2, 4))),
    }


ROUTE_SCALE = 2.827

def reference(tokens, norm_gain, expert_ids, gate_num, node_mask, w_gate, w_up, w_down):
    stream = tokens.astype(jnp.float32)
    inverse_rms = lax.rsqrt(lax.optimization_barrier(jnp.mean(stream * stream, axis=1, keepdims=True)) + 1e-06)
    normed = (stream * inverse_rms * norm_gain.astype(jnp.float32)).astype(jnp.bfloat16)
    is_first = expert_ids % EXP_NODE == 0
    target_node = lax.optimization_barrier(jnp.sum(jnp.where(is_first, expert_ids // EXP_NODE, 0), axis=1)).astype(jnp.int32)
    numerator = lax.optimization_barrier(jnp.sum(jnp.where(is_first, gate_num, 0), axis=1)).astype(jnp.int32)
    allowed = jnp.take_along_axis(node_mask, target_node[:, None], axis=1)[:, 0]
    route_weight = (numerator * allowed).astype(jnp.float32) * (ROUTE_SCALE / DEN)
    sorted_rows = jnp.argsort(target_node, stable=True).astype(jnp.int32)
    node_ids = jnp.arange(N_NODE, dtype=jnp.int32)
    counts = lax.optimization_barrier(jnp.sum((target_node[:, None] == node_ids[None, :]).astype(jnp.int32), axis=0))
    starts = (jnp.cumsum(counts) - counts).astype(jnp.int32)
    window = 2 * TOKENS // N_NODE
    padded = jnp.concatenate([sorted_rows, jnp.zeros((window,), jnp.int32)])

    def one_node(carry, expert_node):
        row_ids = lax.dynamic_slice_in_dim(padded, starts[expert_node], window)
        inside = jnp.arange(window, dtype=jnp.int32) < counts[expert_node]
        inputs = normed[row_ids]
        gate_sum = jnp.dot(inputs, w_gate[expert_node], preferred_element_type=jnp.float32)
        up_sum = jnp.dot(inputs, w_up[expert_node], preferred_element_type=jnp.float32)
        hidden = (jax.nn.silu(gate_sum) * up_sum).astype(jnp.bfloat16)
        result = jnp.dot(hidden, w_down[expert_node], preferred_element_type=jnp.float32).astype(jnp.bfloat16)
        destination = jnp.where(inside, row_ids, TOKENS).astype(jnp.int32)
        carry = carry.at[destination].set(result, mode='drop')
        return (carry, None)
    routed, _ = lax.scan(one_node, jnp.zeros((TOKENS, D), jnp.bfloat16), node_ids)
    return (stream + route_weight[:, None] * routed.astype(jnp.float32)).astype(jnp.bfloat16)
```

```python
import functools

import jax
import jax.numpy as jnp
from jax import lax
from jax.experimental import pallas as pl
from jax.experimental.pallas import tpu as pltpu
from jax.sharding import PartitionSpec as P

EXPERTS = 384
DEN = 4096
ROUTE_SCALE = 2.827
F32 = jnp.float32
BF16 = jnp.bfloat16


def kernel(
    N, C, cap,
    tok, gain, slot_in, weight, wg_hbm, wu_hbm, wd_hbm,
    out,
    normed, held, slots, packed, rows, wgu, wd, partial, sums, hidden, made, back, final,
    w_sem, ss_sem, sr_sem, as_sem, ar_sem, bs_sem, br_sem, cs_sem, cr_sem,
    hs_sem, hr_sem, ds_sem, dr_sem, es_sem, er_sem,
):
    n = lax.axis_index("node")
    c = lax.axis_index("chip")
    T, D = tok.shape
    SW = D // C
    FF = wd.shape[0]
    B = N * cap
    R = B // 4
    K = 2 * C
    GS = partial.shape[0]
    tile = 256 if SW % 256 == 0 else 128

    def loads():
        return (
            pltpu.make_async_copy(wg_hbm.at[0], wgu.at[:, pl.ds(0, FF)], w_sem.at[0]),
            pltpu.make_async_copy(wu_hbm.at[0], wgu.at[:, pl.ds(FF, FF)], w_sem.at[1]),
            pltpu.make_async_copy(wd_hbm.at[0], wd, w_sem.at[2]),
        )

    for copy in loads():
        copy.start()

    barrier = pltpu.get_barrier_semaphore()

    @pl.loop(1, C)
    def _(r):
        pl.semaphore_signal(barrier, inc=1, device_id={"chip": lax.rem(c + r, C)}, device_id_type=pl.DeviceIdType.MESH)

    @pl.loop(1, N)
    def _(r):
        pl.semaphore_signal(barrier, inc=1, device_id={"node": lax.rem(n + r, N)}, device_id_type=pl.DeviceIdType.MESH)

    def remote(src, dst, ssem, rsem, **device):
        return pltpu.make_async_remote_copy(
            src_ref=src, dst_ref=dst, send_sem=ssem, recv_sem=rsem,
            device_id=device, device_id_type=pl.DeviceIdType.MESH,
        )

    def slot_copy(to, src):
        return remote(slot_in, slots.at[src], ss_sem.at[to], sr_sem.at[src], chip=to)

    def a_copy(to, src):
        return remote(normed.at[to], held.at[src], as_sem.at[to], ar_sem.at[src], chip=to)

    def b_copy(b, to, src):
        return remote(
            packed.at[b, pl.ds(pl.multiple_of(to * cap, cap), cap)],
            rows.at[b, pl.ds(pl.multiple_of(src * cap, cap), cap)],
            bs_sem.at[b, to], br_sem.at[b, src], node=to)

    def c_copy(d, k, to):
        return remote(sums.at[d, k], sums.at[d, k], cs_sem.at[d, k], cr_sem.at[d, k], chip=to)

    def place(d, k):
        return lax.div(k, 2), pl.multiple_of(d * 2 * R + lax.rem(k, 2) * R, R)

    def h_copy(d, k, to):
        b, r = place(d, k)
        piece = hidden.at[b, pl.ds(r, R)]
        return remote(piece, piece, hs_sem.at[d, k], hr_sem.at[d, k], chip=to)

    def d_copy(b, to, src):
        return remote(
            made.at[b, pl.ds(pl.multiple_of(to * cap, cap), cap)],
            back.at[b, pl.ds(pl.multiple_of(src * cap, cap), cap)],
            ds_sem.at[b, to], dr_sem.at[b, src], node=to)

    def e_copy(to, src):
        return remote(held.at[to], final.at[src], es_sem.at[to], er_sem.at[src], chip=to)

    def squares(i, acc):
        v = tok[:, pl.ds(pl.multiple_of(i * tile, tile), tile)].astype(F32)
        return acc + v * v

    acc = lax.fori_loop(0, D // tile, squares, jnp.zeros((T, tile), F32))
    inverse = lax.rsqrt(jnp.sum(acc, axis=1, keepdims=True) * (1.0 / D) + 1e-06)

    pl.semaphore_wait(barrier, C + N - 2)

    def normalise(to):
        @pl.loop(0, SW // tile)
        def _(i):
            col = pl.multiple_of(to * SW + i * tile, tile)
            v = tok[:, pl.ds(col, tile)].astype(F32)
            v = v * inverse * gain[:, pl.ds(col, tile)]
            normed[to, :, pl.ds(pl.multiple_of(i * tile, tile), tile)] = v.astype(BF16)

    @pl.loop(1, C)
    def _(r):
        to = lax.rem(c + r, C)
        slot_copy(to, c).start()
        normalise(to)
        a_copy(to, c).start()

    normalise(c)

    def route(source, b, rows_of_slots):
        @pl.loop(0, SW // tile)
        def _(i):
            col = pl.ds(pl.multiple_of(i * tile, tile), tile)
            packed[b, :, col] = jnp.dot(
                rows_of_slots, source[b, :, col], preferred_element_type=F32).astype(BF16)

        @pl.loop(1, N)
        def _(r):
            b_copy(b, lax.rem(n + r, N), n).start()

        own = pl.ds(pl.multiple_of(n * cap, cap), cap)
        rows[b, own, :] = packed[b, own, :]

    def selector(slot_row):
        ids = lax.broadcasted_iota(jnp.int32, (B, T), 0)
        return jnp.where(ids == slot_row, 1.0, 0.0).astype(BF16)

    slots[c] = slot_in[...]
    route(normed, c, selector(slot_in[0:1, :]))

    @pl.loop(1, C)
    def _(r):
        b = lax.rem(c + r, C)
        slot_copy(b, b).wait_recv()
        a_copy(b, b).wait_recv()
        route(held, b, selector(slots[b, 0:1, :]))

    copies = loads()
    copies[0].wait()
    copies[1].wait()
    copies[2].wait()

    ahead = (C - 1) + jnp.maximum(c, C - 1 - c)
    wide = 512
    thin = 16

    @pl.loop(0, K + 2 * (C - 1) + 2)
    def _(t):
        blk = lax.div(t, 2)

        @pl.when((lax.rem(t, 2) == 0) & (blk < C))
        def _():
            @pl.loop(1, N)
            def _(r):
                src = lax.rem(n + r, N)
                b_copy(blk, src, src).wait_recv()

            @pl.loop(0, 2 * FF // wide)
            def _(i):
                col = pl.ds(pl.multiple_of(i * wide, wide), wide)
                partial[lax.rem(blk, GS), :, col] = jnp.dot(
                    rows[blk], wgu[:, col], preferred_element_type=F32)

        for d in (0, 1):
            pos = c if d == 0 else C - 1 - c
            nxt = c + 1 if d == 0 else c - 1
            prv = c - 1 if d == 0 else c + 1
            k = t - pos

            @pl.when((k >= 0) & (k < K) & (pos == 0))
            def _():
                b, r = place(d, k)

                @pl.loop(0, R // thin)
                def _(i):
                    o = pl.multiple_of(i * thin, thin)
                    sums[d, k, pl.ds(o, thin), :] = partial[
                        lax.rem(b, GS), pl.ds(r + o, thin), :].astype(BF16)

                c_copy(d, k, nxt).start()

            @pl.when((k >= 0) & (k < K) & (pos > 0) & (pos < C - 1))
            def _():
                b, r = place(d, k)
                c_copy(d, k, prv).wait_recv()

                @pl.loop(0, R // thin)
                def _(i):
                    o = pl.multiple_of(i * thin, thin)
                    s = sums[d, k, pl.ds(o, thin), :].astype(F32)
                    s += partial[lax.rem(b, GS), pl.ds(r + o, thin), :]
                    sums[d, k, pl.ds(o, thin), :] = s.astype(BF16)

                c_copy(d, k, nxt).start()

            @pl.when((k >= 0) & (k < K) & (pos == C - 1))
            def _():
                b, r = place(d, k)
                c_copy(d, k, prv).wait_recv()

                @pl.loop(0, R // thin)
                def _(i):
                    o = pl.multiple_of(i * thin, thin)
                    s = sums[d, k, pl.ds(o, thin), :].astype(F32)
                    s += partial[lax.rem(b, GS), pl.ds(r + o, thin), :]
                    g, u = s[:, :FF], s[:, FF:]
                    hidden[b, pl.ds(r + o, thin), :] = (
                        g * (1.0 / (1.0 + jnp.exp(-g))) * u).astype(BF16)

                h_copy(d, k, prv).start()

        for d in (0, 1):
            pos = c if d == 0 else C - 1 - c
            nxt = c + 1 if d == 0 else c - 1
            prv = c - 1 if d == 0 else c + 1
            k = t - 2 * (C - 1) + pos

            @pl.when((k >= 0) & (k < K) & (pos < C - 1))
            def _():
                h_copy(d, k, nxt).wait_recv()

                @pl.when(pos > 0)
                def _():
                    h_copy(d, k, prv).start()

        e = t - ahead

        @pl.when((e >= 0) & (lax.rem(e, 2) == 1) & (e < K))
        def _():
            b = lax.div(e, 2)

            @pl.loop(0, SW // tile)
            def _(i):
                col = pl.ds(pl.multiple_of(i * tile, tile), tile)
                made[b, :, col] = jnp.dot(
                    hidden[b], wd[:, col], preferred_element_type=F32).astype(BF16)

            @pl.loop(1, N)
            def _(r):
                d_copy(b, lax.rem(n + r, N), n).start()

            own = pl.ds(pl.multiple_of(n * cap, cap), cap)
            back[b, own, :] = made[b, own, :]

        f = t - ahead - 2

        @pl.when((f >= 0) & (lax.rem(f, 2) == 1) & (f < K))
        def _():
            b = lax.div(f, 2)

            @pl.loop(1, N)
            def _(r):
                src = lax.rem(n + r, N)
                d_copy(b, src, src).wait_recv()

            pick = selector(slots[b, 0:1, :])

            def give(place_to):
                @pl.loop(0, SW // tile)
                def _(i):
                    col = pl.ds(pl.multiple_of(i * tile, tile), tile)
                    place_to[b, :, col] = lax.dot_general(
                        pick, back[b, :, col], (((0,), (0,)), ((), ())),
                        preferred_element_type=F32).astype(BF16)

            @pl.when(b == c)
            def _():
                give(final)

            @pl.when(b != c)
            def _():
                give(held)
                e_copy(b, c).start()

    def finish(src):
        @pl.loop(0, SW // tile)
        def _(i):
            col = pl.ds(pl.multiple_of(src * SW + i * tile, tile), tile)
            v = final[src, :, pl.ds(pl.multiple_of(i * tile, tile), tile)].astype(F32)
            out[:, col] = (tok[:, col].astype(F32) + weight[...] * v).astype(BF16)

    finish(c)

    @pl.loop(1, C)
    def _(r):
        src = lax.rem(c + r, C)
        e_copy(src, src).wait_recv()
        finish(src)

    @pl.loop(1, C)
    def _(r):
        to = lax.rem(c + r, C)
        slot_copy(to, c).wait_send()
        a_copy(to, c).wait_send()
        e_copy(to, c).wait_send()

    @pl.loop(0, C)
    def _(b):
        @pl.loop(1, N)
        def _(r):
            to = lax.rem(n + r, N)
            b_copy(b, to, n).wait_send()
            d_copy(b, to, n).wait_send()

    for d in (0, 1):
        pos = c if d == 0 else C - 1 - c
        nxt = c + 1 if d == 0 else c - 1
        prv = c - 1 if d == 0 else c + 1

        @pl.when(pos < C - 1)
        def _():
            @pl.loop(0, K)
            def _(k):
                c_copy(d, k, nxt).wait_send()

        @pl.when(pos > 0)
        def _():
            @pl.loop(0, K)
            def _(k):
                h_copy(d, k, prv).wait_send()


def body(tokens, norm_gain, expert_ids, gate_num, node_mask, w_gate, w_up, w_down):
    N = lax.axis_size("node")
    C = lax.axis_size("chip")
    T, D = tokens.shape
    SW = D // C
    FF = w_gate.shape[2]
    exp_node = EXPERTS // N
    cap = 2 * T // N
    B = N * cap
    is_first = expert_ids % exp_node == 0
    target = jnp.sum(jnp.where(is_first, expert_ids // exp_node, 0), axis=1)
    numerator = jnp.sum(jnp.where(is_first, gate_num, 0), axis=1)
    at_node = target[:, None] == jnp.arange(N, dtype=jnp.int32)[None, :]
    allowed = jnp.sum(jnp.where(at_node, node_mask, 0), axis=1)
    route_weight = (numerator * allowed).astype(F32) * (ROUTE_SCALE / DEN)
    goes = allowed == 1
    same = (target[:, None] == target[None, :]) & goes[None, :]
    earlier = jnp.arange(T)[None, :] < jnp.arange(T)[:, None]
    position = jnp.sum((same & earlier).astype(jnp.int32), axis=1)
    slot = jnp.where(goes, target * cap + position, B).astype(jnp.int32)
    slot8 = jnp.broadcast_to(slot[None, :], (8, T))
    dma = pltpu.SemaphoreType.DMA
    K = 2 * C
    GS = C // 2 + 1
    vmem = pl.BlockSpec(memory_space=pltpu.VMEM)
    hbm = pl.BlockSpec(memory_space=pl.ANY)
    return pl.pallas_call(
        functools.partial(kernel, N, C, cap),
        out_shape=jax.ShapeDtypeStruct((T, D), BF16),
        in_specs=[vmem] * 4 + [hbm] * 3,
        out_specs=vmem,
        scratch_shapes=[
            pltpu.VMEM((C, T, SW), BF16),
            pltpu.VMEM((C, T, SW), BF16),
            pltpu.VMEM((C, 8, T), jnp.int32),
            pltpu.VMEM((C, B, SW), BF16),
            pltpu.VMEM((C, B, SW), BF16),
            pltpu.VMEM((SW, 2 * FF), BF16),
            pltpu.VMEM((FF, SW), BF16),
            pltpu.VMEM((GS, B, 2 * FF), F32),
            pltpu.VMEM((2, K, B // 4, 2 * FF), BF16),
            pltpu.VMEM((C, B, FF), BF16),
            pltpu.VMEM((C, B, SW), BF16),
            pltpu.VMEM((C, B, SW), BF16),
            pltpu.VMEM((C, T, SW), BF16),
            dma((3,)),
            dma((C,)), dma((C,)), dma((C,)), dma((C,)),
            dma((C, N)), dma((C, N)),
            dma((2, K)), dma((2, K)), dma((2, K)), dma((2, K)),
            dma((C, N)), dma((C, N)),
            dma((C,)), dma((C,)),
        ],
        compiler_params=pltpu.CompilerParams(
            collective_id=0, has_side_effects=True, vmem_limit_bytes=62 * 1024 * 1024
        ),
    )(tokens, norm_gain.reshape(1, D), slot8, route_weight[:, None], w_gate, w_up, w_down)


def solution(mesh):
    placed = (
        P(("grp", "node", "chip"), None),
        P(),
        P(("grp", "node", "chip"), None),
        P(("grp", "node", "chip"), None),
        P(("grp", "node", "chip"), None),
        P("node", "chip", None),
        P("node", "chip", None),
        P("node", None, "chip"),
    )
    return jax.shard_map(
        body,
        mesh=mesh,
        in_specs=placed,
        out_specs=P(("grp", "node", "chip"), None),
        check_vma=False,
    )
```

```python
import functools

import jax
import jax.numpy as jnp
from jax import lax
from jax.experimental import pallas as pl
from jax.experimental.pallas import tpu as pltpu
from jax.sharding import PartitionSpec as P

EXPERTS = 384
DEN = 4096
ROUTE_SCALE = 2.827
F32 = jnp.float32
BF16 = jnp.bfloat16


def kernel(
    N, C, cap,
    tok, gain, slot_in, weight, wg_hbm, wu_hbm, wd_hbm,
    out,
    normed, held, slots, packed, rows, wgu, wd, partial, sums, hidden, made, back, final,
    w_sem, ss_sem, sr_sem, as_sem, ar_sem, bs_sem, br_sem, cs_sem, cr_sem,
    hs_sem, hr_sem, ds_sem, dr_sem, es_sem, er_sem,
):
    n = lax.axis_index("node")
    c = lax.axis_index("chip")
    T, D = tok.shape
    SW = D // C
    FF = wd.shape[0]
    B = N * cap
    R = B // 4
    K = 2 * C
    GS = partial.shape[0]
    tile = 256 if SW % 256 == 0 else 128
    cut = (SW // tile + 1) // 2 * tile
    parts = ((0, cut), (cut, SW - cut))

    def loads():
        return (
            pltpu.make_async_copy(wg_hbm.at[0], wgu.at[:, pl.ds(0, FF)], w_sem.at[0]),
            pltpu.make_async_copy(wu_hbm.at[0], wgu.at[:, pl.ds(FF, FF)], w_sem.at[1]),
            pltpu.make_async_copy(wd_hbm.at[0], wd, w_sem.at[2]),
        )

    for copy in loads():
        copy.start()

    barrier = pltpu.get_barrier_semaphore()

    @pl.loop(1, C)
    def _(r):
        pl.semaphore_signal(barrier, inc=1, device_id={"chip": lax.rem(c + r, C)}, device_id_type=pl.DeviceIdType.MESH)

    @pl.loop(1, N)
    def _(r):
        pl.semaphore_signal(barrier, inc=1, device_id={"node": lax.rem(n + r, N)}, device_id_type=pl.DeviceIdType.MESH)

    def remote(src, dst, ssem, rsem, **device):
        return pltpu.make_async_remote_copy(
            src_ref=src, dst_ref=dst, send_sem=ssem, recv_sem=rsem,
            device_id=device, device_id_type=pl.DeviceIdType.MESH,
        )

    def slot_copy(to, src):
        return remote(slot_in, slots.at[src], ss_sem.at[to], sr_sem.at[src], chip=to)

    def a_copy(h, to, src):
        col = pl.ds(*parts[h])
        return remote(
            normed.at[to, :, col], held.at[src, :, col],
            as_sem.at[h, to], ar_sem.at[h, src], chip=to)

    def b_copy(h, b, to, src):
        col = pl.ds(*parts[h])
        return remote(
            packed.at[b, pl.ds(pl.multiple_of(to * cap, cap), cap), col],
            rows.at[b, pl.ds(pl.multiple_of(src * cap, cap), cap), col],
            bs_sem.at[h, b, to], br_sem.at[h, b, src], node=to)

    def c_copy(d, k, to):
        return remote(sums.at[d, k], sums.at[d, k], cs_sem.at[d, k], cr_sem.at[d, k], chip=to)

    def order(d, i):
        p = lax.div(i, 2)
        return jnp.where(lax.rem(i, 2) == d, p, C - 1 - p)

    def place(d, k):
        return order(d, lax.div(k, 2)), pl.multiple_of(d * 2 * R + lax.rem(k, 2) * R, R)

    low = jnp.where(c < C // 2, 0, 1)

    def kept(d, k):
        i = lax.div(k, 2)
        return lax.rem(jnp.where(low == d, i, i + 1 - 2 * lax.rem(i, 2)), GS)

    def h_copy(d, k, to):
        b, r = place(d, k)
        piece = hidden.at[b, pl.ds(r, R)]
        return remote(piece, piece, hs_sem.at[d, k], hr_sem.at[d, k], chip=to)

    def d_copy(h, b, to, src):
        col = pl.ds(*parts[h])
        return remote(
            made.at[b, pl.ds(pl.multiple_of(to * cap, cap), cap), col],
            back.at[b, pl.ds(pl.multiple_of(src * cap, cap), cap), col],
            ds_sem.at[h, b, to], dr_sem.at[h, b, src], node=to)

    def e_copy(h, to, src):
        col = pl.ds(*parts[h])
        return remote(
            held.at[to, :, col], final.at[src, :, col],
            es_sem.at[h, to], er_sem.at[h, src], chip=to)

    def tiles(h):
        return parts[h][1] // tile

    def at(h, i):
        return pl.multiple_of(parts[h][0] + i * tile, tile)

    def squares(i, acc):
        v = tok[:, pl.ds(pl.multiple_of(i * tile, tile), tile)].astype(F32)
        return acc + v * v

    acc = lax.fori_loop(0, D // tile, squares, jnp.zeros((T, tile), F32))
    inverse = lax.rsqrt(jnp.sum(acc, axis=1, keepdims=True) * (1.0 / D) + 1e-06)

    pl.semaphore_wait(barrier, C + N - 2)

    def normalise(h, to):
        @pl.loop(0, tiles(h))
        def _(i):
            col = pl.multiple_of(to * SW + at(h, i), tile)
            v = tok[:, pl.ds(col, tile)].astype(F32)
            v = v * inverse * gain[:, pl.ds(col, tile)]
            normed[to, :, pl.ds(at(h, i), tile)] = v.astype(BF16)

    @pl.loop(1, C)
    def _(r):
        to = lax.rem(c + r, C)
        slot_copy(to, c).start()
        normalise(0, to)
        a_copy(0, to, c).start()

    @pl.loop(1, C)
    def _(r):
        to = lax.rem(c + r, C)
        normalise(1, to)
        a_copy(1, to, c).start()

    def route(h, source, b, rows_of_slots):
        @pl.loop(0, tiles(h))
        def _(i):
            col = pl.ds(at(h, i), tile)
            packed[b, :, col] = jnp.dot(
                rows_of_slots, source[b, :, col], preferred_element_type=F32).astype(BF16)

        @pl.loop(1, N)
        def _(r):
            b_copy(h, b, lax.rem(n + r, N), n).start()

        own = pl.ds(pl.multiple_of(n * cap, cap), cap)
        part = pl.ds(*parts[h])
        rows[b, own, part] = packed[b, own, part]

    def selector(slot_row):
        ids = lax.broadcasted_iota(jnp.int32, (B, T), 0)
        return jnp.where(ids == slot_row, 1.0, 0.0).astype(BF16)

    slots[c] = slot_in[...]
    for h in (0, 1):
        normalise(h, c)
        route(h, normed, c, selector(slot_in[0:1, :]))

    @pl.loop(1, C)
    def _(r):
        b = lax.rem(c + r, C)
        slot_copy(b, b).wait_recv()
        a_copy(0, b, b).wait_recv()
        route(0, held, b, selector(slots[b, 0:1, :]))

    @pl.loop(1, C)
    def _(r):
        b = lax.rem(c + r, C)
        a_copy(1, b, b).wait_recv()
        route(1, held, b, selector(slots[b, 0:1, :]))

    copies = loads()
    copies[0].wait()
    copies[1].wait()
    copies[2].wait()

    ahead = (C - 1) + jnp.maximum(c, C - 1 - c)
    wide = 512
    thin = 16

    @pl.loop(0, K + 2 * (C - 1) + 2)
    def _(t):
        turn = lax.div(t, 2)

        @pl.when((lax.rem(t, 2) == 0) & (turn < C))
        def _():
            blk = order(low, turn)

            @pl.loop(1, N)
            def _(r):
                src = lax.rem(n + r, N)
                b_copy(0, blk, src, src).wait_recv()
                b_copy(1, blk, src, src).wait_recv()

            @pl.loop(0, 2 * FF // wide)
            def _(i):
                col = pl.ds(pl.multiple_of(i * wide, wide), wide)
                partial[lax.rem(turn, GS), :, col] = jnp.dot(
                    rows[blk], wgu[:, col], preferred_element_type=F32)

        for d in (0, 1):
            pos = c if d == 0 else C - 1 - c
            nxt = c + 1 if d == 0 else c - 1
            prv = c - 1 if d == 0 else c + 1
            k = t - pos

            @pl.when((k >= 0) & (k < K) & (pos == 0))
            def _():
                b, r = place(d, k)

                @pl.loop(0, R // thin)
                def _(i):
                    o = pl.multiple_of(i * thin, thin)
                    sums[d, k, pl.ds(o, thin), :] = partial[
                        kept(d, k), pl.ds(r + o, thin), :].astype(BF16)

                c_copy(d, k, nxt).start()

            @pl.when((k >= 0) & (k < K) & (pos > 0) & (pos < C - 1))
            def _():
                b, r = place(d, k)
                c_copy(d, k, prv).wait_recv()

                @pl.loop(0, R // thin)
                def _(i):
                    o = pl.multiple_of(i * thin, thin)
                    s = sums[d, k, pl.ds(o, thin), :].astype(F32)
                    s += partial[kept(d, k), pl.ds(r + o, thin), :]
                    sums[d, k, pl.ds(o, thin), :] = s.astype(BF16)

                c_copy(d, k, nxt).start()

            @pl.when((k >= 0) & (k < K) & (pos == C - 1))
            def _():
                b, r = place(d, k)
                c_copy(d, k, prv).wait_recv()

                @pl.loop(0, R // thin)
                def _(i):
                    o = pl.multiple_of(i * thin, thin)
                    s = sums[d, k, pl.ds(o, thin), :].astype(F32)
                    s += partial[kept(d, k), pl.ds(r + o, thin), :]
                    g, u = s[:, :FF], s[:, FF:]
                    hidden[b, pl.ds(r + o, thin), :] = (
                        g * (1.0 / (1.0 + jnp.exp(-g))) * u).astype(BF16)

                h_copy(d, k, prv).start()

        for d in (0, 1):
            pos = c if d == 0 else C - 1 - c
            nxt = c + 1 if d == 0 else c - 1
            prv = c - 1 if d == 0 else c + 1
            k = t - 2 * (C - 1) + pos

            @pl.when((k >= 0) & (k < K) & (pos < C - 1))
            def _():
                h_copy(d, k, nxt).wait_recv()

                @pl.when(pos > 0)
                def _():
                    h_copy(d, k, prv).start()

        e = t - ahead

        @pl.when((e >= 0) & (lax.rem(e, 4) == 3) & (e < K))
        def _():
            pair = lax.div(e, 4)
            for h in (0, 1):
                @pl.loop(0, 2)
                def _(m):
                    b = order(0, 2 * pair + m)

                    @pl.loop(0, tiles(h))
                    def _(i):
                        col = pl.ds(at(h, i), tile)
                        made[b, :, col] = jnp.dot(
                            hidden[b], wd[:, col], preferred_element_type=F32).astype(BF16)

                    @pl.loop(1, N)
                    def _(r):
                        d_copy(h, b, lax.rem(n + r, N), n).start()

                    own = pl.ds(pl.multiple_of(n * cap, cap), cap)
                    part = pl.ds(*parts[h])
                    back[b, own, part] = made[b, own, part]

        f = t - ahead - 2

        @pl.when((f >= 0) & (lax.rem(f, 4) == 3) & (f < K))
        def _():
            pair = lax.div(f, 4)
            for h in (0, 1):
                @pl.loop(0, 2)
                def _(m):
                    b = order(0, 2 * pair + m)

                    @pl.loop(1, N)
                    def _(r):
                        src = lax.rem(n + r, N)
                        d_copy(h, b, src, src).wait_recv()

                    pick = selector(slots[b, 0:1, :])

                    def give(place_to):
                        @pl.loop(0, tiles(h))
                        def _(i):
                            col = pl.ds(at(h, i), tile)
                            place_to[b, :, col] = lax.dot_general(
                                pick, back[b, :, col], (((0,), (0,)), ((), ())),
                                preferred_element_type=F32).astype(BF16)

                    @pl.when(b == c)
                    def _():
                        give(final)

                    @pl.when(b != c)
                    def _():
                        give(held)
                        e_copy(h, b, c).start()

    def finish(h, src):
        @pl.loop(0, tiles(h))
        def _(i):
            col = pl.ds(pl.multiple_of(src * SW + at(h, i), tile), tile)
            v = final[src, :, pl.ds(at(h, i), tile)].astype(F32)
            out[:, col] = (tok[:, col].astype(F32) + weight[...] * v).astype(BF16)

    for h in (0, 1):
        finish(h, c)

        @pl.loop(1, C)
        def _(r):
            src = lax.rem(c + r, C)
            e_copy(h, src, src).wait_recv()
            finish(h, src)

    @pl.loop(1, C)
    def _(r):
        to = lax.rem(c + r, C)
        slot_copy(to, c).wait_send()
        for h in (0, 1):
            a_copy(h, to, c).wait_send()
            e_copy(h, to, c).wait_send()

    @pl.loop(0, C)
    def _(b):
        @pl.loop(1, N)
        def _(r):
            to = lax.rem(n + r, N)
            for h in (0, 1):
                b_copy(h, b, to, n).wait_send()
                d_copy(h, b, to, n).wait_send()

    for d in (0, 1):
        pos = c if d == 0 else C - 1 - c
        nxt = c + 1 if d == 0 else c - 1
        prv = c - 1 if d == 0 else c + 1

        @pl.when(pos < C - 1)
        def _():
            @pl.loop(0, K)
            def _(k):
                c_copy(d, k, nxt).wait_send()

        @pl.when(pos > 0)
        def _():
            @pl.loop(0, K)
            def _(k):
                h_copy(d, k, prv).wait_send()


def body(tokens, norm_gain, expert_ids, gate_num, node_mask, w_gate, w_up, w_down):
    N = lax.axis_size("node")
    C = lax.axis_size("chip")
    T, D = tokens.shape
    SW = D // C
    FF = w_gate.shape[2]
    exp_node = EXPERTS // N
    cap = 2 * T // N
    B = N * cap
    is_first = expert_ids % exp_node == 0
    target = jnp.sum(jnp.where(is_first, expert_ids // exp_node, 0), axis=1)
    numerator = jnp.sum(jnp.where(is_first, gate_num, 0), axis=1)
    at_node = target[:, None] == jnp.arange(N, dtype=jnp.int32)[None, :]
    allowed = jnp.sum(jnp.where(at_node, node_mask, 0), axis=1)
    route_weight = (numerator * allowed).astype(F32) * (ROUTE_SCALE / DEN)
    goes = allowed == 1
    same = (target[:, None] == target[None, :]) & goes[None, :]
    earlier = jnp.arange(T)[None, :] < jnp.arange(T)[:, None]
    position = jnp.sum((same & earlier).astype(jnp.int32), axis=1)
    slot = jnp.where(goes, target * cap + position, B).astype(jnp.int32)
    slot8 = jnp.broadcast_to(slot[None, :], (8, T))
    dma = pltpu.SemaphoreType.DMA
    K = 2 * C
    GS = C // 2 + 2
    vmem = pl.BlockSpec(memory_space=pltpu.VMEM)
    hbm = pl.BlockSpec(memory_space=pl.ANY)
    return pl.pallas_call(
        functools.partial(kernel, N, C, cap),
        out_shape=jax.ShapeDtypeStruct((T, D), BF16),
        in_specs=[vmem] * 4 + [hbm] * 3,
        out_specs=vmem,
        scratch_shapes=[
            pltpu.VMEM((C, T, SW), BF16),
            pltpu.VMEM((C, T, SW), BF16),
            pltpu.VMEM((C, 8, T), jnp.int32),
            pltpu.VMEM((C, B, SW), BF16),
            pltpu.VMEM((C, B, SW), BF16),
            pltpu.VMEM((SW, 2 * FF), BF16),
            pltpu.VMEM((FF, SW), BF16),
            pltpu.VMEM((GS, B, 2 * FF), F32),
            pltpu.VMEM((2, K, B // 4, 2 * FF), BF16),
            pltpu.VMEM((C, B, FF), BF16),
            pltpu.VMEM((C, B, SW), BF16),
            pltpu.VMEM((C, B, SW), BF16),
            pltpu.VMEM((C, T, SW), BF16),
            dma((3,)),
            dma((C,)), dma((C,)), dma((2, C)), dma((2, C)),
            dma((2, C, N)), dma((2, C, N)),
            dma((2, K)), dma((2, K)), dma((2, K)), dma((2, K)),
            dma((2, C, N)), dma((2, C, N)),
            dma((2, C)), dma((2, C)),
        ],
        compiler_params=pltpu.CompilerParams(
            collective_id=0, has_side_effects=True, vmem_limit_bytes=62 * 1024 * 1024
        ),
    )(tokens, norm_gain.reshape(1, D), slot8, route_weight[:, None], w_gate, w_up, w_down)


def solution(mesh):
    placed = (
        P(("grp", "node", "chip"), None),
        P(),
        P(("grp", "node", "chip"), None),
        P(("grp", "node", "chip"), None),
        P(("grp", "node", "chip"), None),
        P("node", "chip", None),
        P("node", "chip", None),
        P("node", None, "chip"),
    )
    return jax.shard_map(
        body,
        mesh=mesh,
        in_specs=placed,
        out_specs=P(("grp", "node", "chip"), None),
        check_vma=False,
    )
```

```python
import functools

import jax
import jax.numpy as jnp
from jax import lax
from jax.experimental import pallas as pl
from jax.experimental.pallas import tpu as pltpu
from jax.sharding import PartitionSpec as P

EXPERTS = 384
DEN = 4096
ROUTE_SCALE = 2.827
F32 = jnp.float32
BF16 = jnp.bfloat16
PARTS = 4


def kernel(
    N, C, cap,
    tok, gain, slot_in, weight, wg_hbm, wu_hbm, wd_hbm,
    out,
    normed, held, slots, packed, rows, wgu, wd, partial, sums, hidden, made, back, final,
    w_sem, ss_sem, sr_sem, as_sem, ar_sem, bs_sem, br_sem, cs_sem, cr_sem,
    hs_sem, hr_sem, ds_sem, dr_sem, es_sem, er_sem,
):
    n = lax.axis_index("node")
    c = lax.axis_index("chip")
    T, D = tok.shape
    SW = D // C
    FF = wd.shape[0]
    B = N * cap
    R = B // 4
    K = 2 * C
    GS = partial.shape[0]
    tile = 256 if SW % 256 == 0 else 128
    step = -(-SW // tile // PARTS) * tile
    parts = [(o, min(step, SW - o)) for o in range(0, SW, step)]
    every = range(len(parts))

    def loads():
        return (
            pltpu.make_async_copy(wg_hbm.at[0], wgu.at[:, pl.ds(0, FF)], w_sem.at[0]),
            pltpu.make_async_copy(wu_hbm.at[0], wgu.at[:, pl.ds(FF, FF)], w_sem.at[1]),
            pltpu.make_async_copy(wd_hbm.at[0], wd, w_sem.at[2]),
        )

    for copy in loads():
        copy.start()

    barrier = pltpu.get_barrier_semaphore()

    @pl.loop(1, C)
    def _(r):
        pl.semaphore_signal(barrier, inc=1, device_id={"chip": lax.rem(c + r, C)}, device_id_type=pl.DeviceIdType.MESH)

    @pl.loop(1, N)
    def _(r):
        pl.semaphore_signal(barrier, inc=1, device_id={"node": lax.rem(n + r, N)}, device_id_type=pl.DeviceIdType.MESH)

    def remote(src, dst, ssem, rsem, **device):
        return pltpu.make_async_remote_copy(
            src_ref=src, dst_ref=dst, send_sem=ssem, recv_sem=rsem,
            device_id=device, device_id_type=pl.DeviceIdType.MESH,
        )

    def slot_copy(to, src):
        return remote(slot_in, slots.at[src], ss_sem.at[to], sr_sem.at[src], chip=to)

    def a_copy(h, to, src):
        col = pl.ds(*parts[h])
        return remote(
            normed.at[to, :, col], held.at[src, :, col],
            as_sem.at[h, to], ar_sem.at[h, src], chip=to)

    def b_copy(h, b, to, src):
        col = pl.ds(*parts[h])
        return remote(
            packed.at[b, pl.ds(pl.multiple_of(to * cap, cap), cap), col],
            rows.at[b, pl.ds(pl.multiple_of(src * cap, cap), cap), col],
            bs_sem.at[h, b, to], br_sem.at[h, b, src], node=to)

    def c_copy(d, k, to):
        return remote(sums.at[d, k], sums.at[d, k], cs_sem.at[d, k], cr_sem.at[d, k], chip=to)

    def order(d, i):
        p = lax.div(i, 2)
        return jnp.where(lax.rem(i, 2) == d, p, C - 1 - p)

    def place(d, k):
        return order(d, lax.div(k, 2)), pl.multiple_of(d * 2 * R + lax.rem(k, 2) * R, R)

    low = jnp.where(c < C // 2, 0, 1)

    def kept(d, k):
        i = lax.div(k, 2)
        return lax.rem(jnp.where(low == d, i, i + 1 - 2 * lax.rem(i, 2)), GS)

    def h_copy(d, k, to):
        b, r = place(d, k)
        piece = hidden.at[b, pl.ds(r, R)]
        return remote(piece, piece, hs_sem.at[d, k], hr_sem.at[d, k], chip=to)

    def d_copy(h, b, to, src):
        col = pl.ds(*parts[h])
        return remote(
            made.at[b, pl.ds(pl.multiple_of(to * cap, cap), cap), col],
            back.at[b, pl.ds(pl.multiple_of(src * cap, cap), cap), col],
            ds_sem.at[h, b, to], dr_sem.at[h, b, src], node=to)

    def e_copy(h, to, src):
        col = pl.ds(*parts[h])
        return remote(
            held.at[to, :, col], final.at[src, :, col],
            es_sem.at[h, to], er_sem.at[h, src], chip=to)

    def tiles(h):
        return parts[h][1] // tile

    def at(h, i):
        return pl.multiple_of(parts[h][0] + i * tile, tile)

    def squares(i, acc):
        v = tok[:, pl.ds(pl.multiple_of(i * tile, tile), tile)].astype(F32)
        return acc + v * v

    acc = lax.fori_loop(0, D // tile, squares, jnp.zeros((T, tile), F32))
    inverse = lax.rsqrt(jnp.sum(acc, axis=1, keepdims=True) * (1.0 / D) + 1e-06)

    pl.semaphore_wait(barrier, C + N - 2)

    def normalise(h, to):
        @pl.loop(0, tiles(h))
        def _(i):
            col = pl.multiple_of(to * SW + at(h, i), tile)
            v = tok[:, pl.ds(col, tile)].astype(F32)
            v = v * inverse * gain[:, pl.ds(col, tile)]
            normed[to, :, pl.ds(at(h, i), tile)] = v.astype(BF16)

    @pl.loop(1, C)
    def _(r):
        to = lax.rem(c + r, C)
        slot_copy(to, c).start()
        normalise(0, to)
        a_copy(0, to, c).start()

    for h in every[1:]:
        @pl.loop(1, C)
        def _(r):
            to = lax.rem(c + r, C)
            normalise(h, to)
            a_copy(h, to, c).start()

    def route(h, source, b, rows_of_slots):
        @pl.loop(0, tiles(h))
        def _(i):
            col = pl.ds(at(h, i), tile)
            packed[b, :, col] = jnp.dot(
                rows_of_slots, source[b, :, col], preferred_element_type=F32).astype(BF16)

        @pl.loop(1, N)
        def _(r):
            b_copy(h, b, lax.rem(n + r, N), n).start()

        own = pl.ds(pl.multiple_of(n * cap, cap), cap)
        part = pl.ds(*parts[h])
        rows[b, own, part] = packed[b, own, part]

    def selector(slot_row):
        ids = lax.broadcasted_iota(jnp.int32, (B, T), 0)
        return jnp.where(ids == slot_row, 1.0, 0.0).astype(BF16)

    slots[c] = slot_in[...]
    for h in every:
        normalise(h, c)
        route(h, normed, c, selector(slot_in[0:1, :]))

    def bring(b):
        @pl.when(b != c)
        def _():
            slot_copy(b, b).wait_recv()
            pick = selector(slots[b, 0:1, :])
            for h in every:
                a_copy(h, b, b).wait_recv()
                route(h, held, b, pick)

    bring(order(low, 0))

    copies = loads()
    copies[0].wait()
    copies[1].wait()
    copies[2].wait()

    ahead = (C - 1) + jnp.maximum(c, C - 1 - c)
    wide = 512
    thin = 16

    @pl.loop(0, K + 2 * (C - 1) + 2)
    def _(t):
        turn = lax.div(t, 2)

        @pl.when((lax.rem(t, 2) == 0) & (turn < C))
        def _():
            blk = order(low, turn)

            @pl.loop(1, N)
            def _(r):
                src = lax.rem(n + r, N)
                for h in every:
                    b_copy(h, blk, src, src).wait_recv()

            @pl.loop(0, 2 * FF // wide)
            def _(i):
                col = pl.ds(pl.multiple_of(i * wide, wide), wide)
                partial[lax.rem(turn, GS), :, col] = jnp.dot(
                    rows[blk], wgu[:, col], preferred_element_type=F32)

        for d in (0, 1):
            pos = c if d == 0 else C - 1 - c
            nxt = c + 1 if d == 0 else c - 1
            prv = c - 1 if d == 0 else c + 1
            k = t - pos

            @pl.when((k >= 0) & (k < K) & (pos == 0))
            def _():
                b, r = place(d, k)

                @pl.loop(0, R // thin)
                def _(i):
                    o = pl.multiple_of(i * thin, thin)
                    sums[d, k, pl.ds(o, thin), :] = partial[
                        kept(d, k), pl.ds(r + o, thin), :].astype(BF16)

                c_copy(d, k, nxt).start()

            @pl.when((k >= 0) & (k < K) & (pos > 0) & (pos < C - 1))
            def _():
                b, r = place(d, k)
                c_copy(d, k, prv).wait_recv()

                @pl.loop(0, R // thin)
                def _(i):
                    o = pl.multiple_of(i * thin, thin)
                    s = sums[d, k, pl.ds(o, thin), :].astype(F32)
                    s += partial[kept(d, k), pl.ds(r + o, thin), :]
                    sums[d, k, pl.ds(o, thin), :] = s.astype(BF16)

                c_copy(d, k, nxt).start()

            @pl.when((k >= 0) & (k < K) & (pos == C - 1))
            def _():
                b, r = place(d, k)
                c_copy(d, k, prv).wait_recv()

                @pl.loop(0, R // thin)
                def _(i):
                    o = pl.multiple_of(i * thin, thin)
                    s = sums[d, k, pl.ds(o, thin), :].astype(F32)
                    s += partial[kept(d, k), pl.ds(r + o, thin), :]
                    g, u = s[:, :FF], s[:, FF:]
                    hidden[b, pl.ds(r + o, thin), :] = (
                        g * (1.0 / (1.0 + jnp.exp(-g))) * u).astype(BF16)

                h_copy(d, k, prv).start()

        for d in (0, 1):
            pos = c if d == 0 else C - 1 - c
            nxt = c + 1 if d == 0 else c - 1
            prv = c - 1 if d == 0 else c + 1
            k = t - 2 * (C - 1) + pos

            @pl.when((k >= 0) & (k < K) & (pos < C - 1))
            def _():
                h_copy(d, k, nxt).wait_recv()

                @pl.when(pos > 0)
                def _():
                    h_copy(d, k, prv).start()

        @pl.when((lax.rem(t, 2) == 0) & (turn < C - 1))
        def _():
            bring(order(low, turn + 1))

        e = t - ahead

        @pl.when((e >= 0) & (lax.rem(e, 4) == 3) & (e < K))
        def _():
            pair = lax.div(e, 4)
            for h in every:
                @pl.loop(0, 2)
                def _(m):
                    b = order(0, 2 * pair + m)

                    @pl.loop(0, tiles(h))
                    def _(i):
                        col = pl.ds(at(h, i), tile)
                        made[b, :, col] = jnp.dot(
                            hidden[b], wd[:, col], preferred_element_type=F32).astype(BF16)

                    @pl.loop(1, N)
                    def _(r):
                        d_copy(h, b, lax.rem(n + r, N), n).start()

                    own = pl.ds(pl.multiple_of(n * cap, cap), cap)
                    part = pl.ds(*parts[h])
                    back[b, own, part] = made[b, own, part]

        f = t - ahead - 2

        @pl.when((f >= 0) & (lax.rem(f, 4) == 3) & (f < K))
        def _():
            pair = lax.div(f, 4)
            for h in every:
                @pl.loop(0, 2)
                def _(m):
                    b = order(0, 2 * pair + m)

                    @pl.loop(1, N)
                    def _(r):
                        src = lax.rem(n + r, N)
                        d_copy(h, b, src, src).wait_recv()

                    pick = selector(slots[b, 0:1, :])

                    def give(place_to):
                        @pl.loop(0, tiles(h))
                        def _(i):
                            col = pl.ds(at(h, i), tile)
                            place_to[b, :, col] = lax.dot_general(
                                pick, back[b, :, col], (((0,), (0,)), ((), ())),
                                preferred_element_type=F32).astype(BF16)

                    @pl.when(b == c)
                    def _():
                        give(final)

                    @pl.when(b != c)
                    def _():
                        give(held)
                        e_copy(h, b, c).start()

    def finish(h, src):
        @pl.loop(0, tiles(h))
        def _(i):
            col = pl.ds(pl.multiple_of(src * SW + at(h, i), tile), tile)
            v = final[src, :, pl.ds(at(h, i), tile)].astype(F32)
            out[:, col] = (tok[:, col].astype(F32) + weight[...] * v).astype(BF16)

    for h in every:
        finish(h, c)

        @pl.loop(1, C)
        def _(r):
            src = lax.rem(c + r, C)
            e_copy(h, src, src).wait_recv()
            finish(h, src)

    @pl.loop(1, C)
    def _(r):
        to = lax.rem(c + r, C)
        slot_copy(to, c).wait_send()
        for h in every:
            a_copy(h, to, c).wait_send()
            e_copy(h, to, c).wait_send()

    @pl.loop(0, C)
    def _(b):
        @pl.loop(1, N)
        def _(r):
            to = lax.rem(n + r, N)
            for h in every:
                b_copy(h, b, to, n).wait_send()
                d_copy(h, b, to, n).wait_send()

    for d in (0, 1):
        pos = c if d == 0 else C - 1 - c
        nxt = c + 1 if d == 0 else c - 1
        prv = c - 1 if d == 0 else c + 1

        @pl.when(pos < C - 1)
        def _():
            @pl.loop(0, K)
            def _(k):
                c_copy(d, k, nxt).wait_send()

        @pl.when(pos > 0)
        def _():
            @pl.loop(0, K)
            def _(k):
                h_copy(d, k, prv).wait_send()


def body(tokens, norm_gain, expert_ids, gate_num, node_mask, w_gate, w_up, w_down):
    N = lax.axis_size("node")
    C = lax.axis_size("chip")
    T, D = tokens.shape
    SW = D // C
    FF = w_gate.shape[2]
    exp_node = EXPERTS // N
    cap = 2 * T // N
    B = N * cap
    is_first = expert_ids % exp_node == 0
    target = jnp.sum(jnp.where(is_first, expert_ids // exp_node, 0), axis=1)
    numerator = jnp.sum(jnp.where(is_first, gate_num, 0), axis=1)
    at_node = target[:, None] == jnp.arange(N, dtype=jnp.int32)[None, :]
    allowed = jnp.sum(jnp.where(at_node, node_mask, 0), axis=1)
    route_weight = (numerator * allowed).astype(F32) * (ROUTE_SCALE / DEN)
    goes = allowed == 1
    same = (target[:, None] == target[None, :]) & goes[None, :]
    earlier = jnp.arange(T)[None, :] < jnp.arange(T)[:, None]
    position = jnp.sum((same & earlier).astype(jnp.int32), axis=1)
    slot = jnp.where(goes, target * cap + position, B).astype(jnp.int32)
    slot8 = jnp.broadcast_to(slot[None, :], (8, T))
    dma = pltpu.SemaphoreType.DMA
    K = 2 * C
    GS = C // 2 + 2
    vmem = pl.BlockSpec(memory_space=pltpu.VMEM)
    hbm = pl.BlockSpec(memory_space=pl.ANY)
    return pl.pallas_call(
        functools.partial(kernel, N, C, cap),
        out_shape=jax.ShapeDtypeStruct((T, D), BF16),
        in_specs=[vmem] * 4 + [hbm] * 3,
        out_specs=vmem,
        scratch_shapes=[
            pltpu.VMEM((C, T, SW), BF16),
            pltpu.VMEM((C, T, SW), BF16),
            pltpu.VMEM((C, 8, T), jnp.int32),
            pltpu.VMEM((C, B, SW), BF16),
            pltpu.VMEM((C, B, SW), BF16),
            pltpu.VMEM((SW, 2 * FF), BF16),
            pltpu.VMEM((FF, SW), BF16),
            pltpu.VMEM((GS, B, 2 * FF), F32),
            pltpu.VMEM((2, K, B // 4, 2 * FF), BF16),
            pltpu.VMEM((C, B, FF), BF16),
            pltpu.VMEM((C, B, SW), BF16),
            pltpu.VMEM((C, B, SW), BF16),
            pltpu.VMEM((C, T, SW), BF16),
            dma((3,)),
            dma((C,)), dma((C,)), dma((PARTS, C)), dma((PARTS, C)),
            dma((PARTS, C, N)), dma((PARTS, C, N)),
            dma((2, K)), dma((2, K)), dma((2, K)), dma((2, K)),
            dma((PARTS, C, N)), dma((PARTS, C, N)),
            dma((PARTS, C)), dma((PARTS, C)),
        ],
        compiler_params=pltpu.CompilerParams(
            collective_id=0, has_side_effects=True, vmem_limit_bytes=62 * 1024 * 1024
        ),
    )(tokens, norm_gain.reshape(1, D), slot8, route_weight[:, None], w_gate, w_up, w_down)


def solution(mesh):
    placed = (
        P(("grp", "node", "chip"), None),
        P(),
        P(("grp", "node", "chip"), None),
        P(("grp", "node", "chip"), None),
        P(("grp", "node", "chip"), None),
        P("node", "chip", None),
        P("node", "chip", None),
        P("node", None, "chip"),
    )
    return jax.shard_map(
        body,
        mesh=mesh,
        in_specs=placed,
        out_specs=P(("grp", "node", "chip"), None),
        check_vma=False,
    )
```
